512 devices in a mesh: tm: 128 (over y, z, core), space: 4 (over x).
Axes of the slice: x: 4, y: 8, z: 8, core: 2. Of those that a mesh axis runs over, the one named last changes fastest.
Arguments:
- source: float32 [128, 32, 128, 128], P('tm', 'space'), may hold values from -8 to 8
- conductivity: float32 [32, 128, 128], P('space'), may hold values from 0.5 to 4
Outputs:
- solution: float32 [128, 32, 128, 128], P('tm', 'space')
- final_defect: float32 [128, 32, 128, 128], P('tm', 'space')
The draws below stay inside these ranges and needn't reach their ends.
All inputs are finite; a program needn't handle non-finite values.
Results may differ from the reference program's by a relative error of at most 0.000034.
Values sent between devices are 32-bit elements; how exact they have to be, the bound alone decides.
No kernel may reach another device: no remote copies, remote signals or barrier semaphores. Data moves between devices by JAX's collectives and lax.ppermute only.
A program may use at most 64 MiB of HBM per device.

```python
import math
import jax
import jax.numpy as jnp

NX = 128
NY = 128
NU = 2
NC = 4
NZ = 32
NT = 128


def level_of(rng, extent, split, smallest, high):
    gain, own = 1.0, jax.random.fold_in(rng, 6)
    for position, parts in split:
        draws = jnp.exp(jax.random.uniform(jax.random.fold_in(own, position), (parts,), jnp.float32, smallest / len(split), high / len(split)))
        gain = gain * jnp.repeat(draws, extent[position] // parts).reshape([-1 if axis == position else 1 for axis in range(len(extent))])
    return gain


def normal_values(key, extent, spread, reach, split=(), held_as=jnp.bfloat16):
    drawn = jax.random.normal(key, extent, jnp.float32) * spread
    if len(split) > 0:
        drawn = level_of(key, extent, split, -0.22, 0.18) * drawn
    return jnp.clip(drawn, min=-reach, max=reach).astype(held_as)


def setup_inputs(seed: int = 0) -> dict:
    key_of = jax.random.split(jax.random.key(seed), 3)
    source = normal_values(key_of[0], (NT, NZ, NX, NY), 1.0, 8.0, ((0, 128), (1, 4)), jnp.float32)
    conductivity = jnp.clip(jnp.exp(math.log(4.0) - 2.0794415 * jax.random.uniform(key_of[1], (NZ, NX, NY), jnp.float32) ** level_of(key_of[1], (NZ, NX, NY), ((0, 4),), -0.2, 0.2)), 0.5, 4.0)
    return {"source": source, "conductivity": conductivity}


OMEGA = 0.8
FINE = (1.0, 1.0, 1.0)
COARSE = (0.25, 0.25, 1.0)


def stencil(padded, weights):
    weight_z, weight_x, weight_y = weights
    centre = padded[..., 1:-1, :, :]
    widths = [(0, 0)] * (centre.ndim - 2) + [(1, 1), (1, 1)]
    framed = jnp.pad(centre, widths)
    along_z = 2.0 * centre - padded[..., 2:, :, :] - padded[..., :-2, :, :]
    along_x = 2.0 * centre - framed[..., 2:, 1:-1] - framed[..., :-2, 1:-1]
    along_y = 2.0 * centre - framed[..., 1:-1, 2:] - framed[..., 1:-1, :-2]
    return weight_z * along_z + weight_x * along_x + weight_y * along_y


def defect(current, right_side, earlier, padded, conduct, stretch, weights):
    applied = current + stretch * conduct * stencil(padded, weights)
    return right_side + earlier - applied


def relaxed(current, right_side, earlier, padded, conduct, stretch, weights):
    weight_sum = 2.0 * (weights[0] + weights[1] + weights[2])
    diagonal = 1.0 + stretch * conduct * weight_sum
    return current + OMEGA * defect(current, right_side, earlier, padded, conduct, stretch, weights) / diagonal


def coarsen(values):
    return 0.25 * ((values[..., 0::2, 0::2, :] + values[..., 1::2, 0::2, :]) + (values[..., 0::2, 1::2, :] + values[..., 1::2, 1::2, :]))


def refine(values):
    return jnp.repeat(jnp.repeat(values, 2, axis=-3), 2, axis=-2)


def pad_planes(values):
    return jnp.pad(values, [(0, 0)] * (values.ndim - 3) + [(1, 1), (0, 0), (0, 0)])


def time_before(values):
    return jnp.concatenate([jnp.zeros_like(values[:1]), values[:-1]], 0)


def smooth(current, right_side, conduct, stretch, weights, repeats):
    for turn_index in range(repeats):
        current = relaxed(current, right_side, time_before(current), pad_planes(current), conduct, stretch, weights)
    return current


def level_defect(current, right_side, conduct, stretch, weights):
    return defect(current, right_side, time_before(current), pad_planes(current), conduct, stretch, weights)


def reference(source, conductivity):
    solution = smooth(jnp.zeros_like(source), source, conductivity, 1.0, FINE, NU)
    defect_fine = level_defect(solution, source, conductivity, 1.0, FINE)
    middle_rhs = defect_fine[0::2] + defect_fine[1::2]
    middle = smooth(jnp.zeros_like(middle_rhs), middle_rhs, conductivity, 2.0, FINE, NU)
    middle_defect = level_defect(middle, middle_rhs, conductivity, 2.0, FINE)
    summed = middle_defect[0::2] + middle_defect[1::2]
    coarse_rhs = coarsen(summed)
    coarse_cond = coarsen(conductivity)
    coarse = smooth(jnp.zeros_like(coarse_rhs), coarse_rhs, coarse_cond, 4.0, COARSE, NC)
    middle = middle + jnp.repeat(refine(coarse), 2, axis=0)
    middle = smooth(middle, middle_rhs, conductivity, 2.0, FINE, NU)
    solution = solution + jnp.repeat(middle, 2, axis=0)
    solution = smooth(solution, source, conductivity, 1.0, FINE, NU)
    final_defect = level_defect(solution, source, conductivity, 1.0, FINE)
    return solution, final_defect
```

```python
import jax
import jax.numpy as jnp
from jax import lax
from jax.sharding import PartitionSpec as P

OMEGA = 0.8
FINE = (1.0, 1.0, 1.0)
COARSE = (0.25, 0.25, 1.0)
HALF = 64
ROWS = 80
WIDE = 4


def shifted(value, by):
    peers = lax.axis_size("tm")
    return lax.ppermute(value, "tm", [(i, i + by) for i in range(peers) if 0 <= i + by < peers])


def flipped(value, mask):
    peers = lax.axis_size("tm")
    return lax.ppermute(value, "tm", [(i, i ^ mask) for i in range(peers)])


def crossed(value):
    peers = lax.axis_size("tm")
    pairs = [(i, i + (2 if i & 2 else 6)) for i in range(peers)]
    return lax.ppermute(value, "tm", [(i, j) for i, j in pairs if j < peers])


def faces(value, width, dim=0):
    peers, length = lax.axis_size("space"), value.shape[dim]
    up = [(i, i + 1) for i in range(peers - 1)]
    before = lax.ppermute(lax.slice_in_dim(value, length - width, length, axis=dim), "space", up)
    after = lax.ppermute(
        lax.slice_in_dim(value, 0, width, axis=dim), "space", [(j, i) for i, j in up]
    )
    return before, after


def framed(value, width, dim=0):
    before, after = faces(value, width, dim)
    return jnp.concatenate([before, value, after], axis=dim)


def stencil(v, weights=FINE):
    a, b, d = weights
    m = v[..., 1:-1, :, :]
    lead = [(0, 0)] * (v.ndim - 2)
    px = jnp.pad(m, lead + [(1, 1), (0, 0)])
    py = jnp.pad(m, lead + [(0, 0), (1, 1)])
    return (
        2.0 * (a + b + d) * m
        - a * (v[..., 2:, :, :] + v[..., :-2, :, :])
        - b * (px[..., 2:, :] + px[..., :-2, :])
        - d * (py[..., 2:] + py[..., :-2])
    )


def inner(v, n=1):
    return v[..., n:-n, :, :]


def applied(v, c, weights=FINE):
    return inner(v) + c * stencil(v, weights)


def pair_matrix(rows):
    i = lax.broadcasted_iota(jnp.int32, (rows // 2, rows), 0)
    j = lax.broadcasted_iota(jnp.int32, (rows // 2, rows), 1)
    return (j // 2 == i).astype(jnp.float32)


def coarsen(v):
    z = v[..., 0::2, :, :] + v[..., 1::2, :, :]
    rows = z.shape[-2]
    return 0.25 * jnp.einsum(
        "ij,...jy->...iy", pair_matrix(rows), z, precision=lax.Precision.HIGHEST
    )


def refine(v):
    rows = v.shape[-2] * 2
    wide = jnp.einsum(
        "ij,...iy->...jy", pair_matrix(rows), v, precision=lax.Precision.HIGHEST
    )
    return jnp.repeat(wide, 2, axis=-3)


def body(source, conductivity):
    me = lax.axis_index("tm")
    core = me % 2
    odd_chip = (me // 2) % 2 == 1
    low = core == 0
    planes, rows, _ = conductivity.shape
    k = WIDE

    def window(v, keep):
        return jnp.where(keep, v[:, :ROWS], v[:, rows - ROWS :])

    mine = window(source[0], low)
    got = flipped(window(source[0], ~low), 1)
    even, odd = jnp.where(low, mine, got), jnp.where(low, got, mine)
    bundle = framed(jnp.stack([even, odd, window(conductivity, low)]), k, 1)
    prior_odd = shifted(odd, 2)
    g, cond = bundle[:2], bundle[2]
    d0 = OMEGA / (1.0 + 6.0 * cond)
    d1 = OMEGA / (1.0 + 12.0 * cond)

    c14, c12 = inner(cond, 1), inner(cond, 2)
    u1 = d0 * g
    rest = inner(u1) + inner(d0) * (inner(g) - applied(u1, c14))
    hop = d0 * u1
    odd2 = rest[1] + inner(hop[0])
    w = inner(odd2) - c12 * stencil(inner(hop[1]))
    local = inner(g[0] + g[1], 2) + inner(rest[0]) - applied(rest[0] + odd2, c12)
    g1 = local + shifted(w, 2)

    c10, c8 = 2.0 * inner(cond, 3), 2.0 * inner(cond, 4)
    m1 = inner(d1, 2) * g1
    rest1 = inner(m1) + inner(d1, 3) * (inner(g1) - applied(m1, c10))
    hop1 = inner(d1, 3) * inner(m1)
    own = inner(g1, 2) - applied(rest1, c8)
    nxt = inner(rest1) - applied(hop1, c8)
    carry = inner(hop1)
    pair = coarsen(
        jnp.stack([own + jnp.where(odd_chip, 0.0, nxt), carry + jnp.where(odd_chip, nxt, 0.0)])
    )
    f0, f1 = pair[0], pair[1]
    g2 = (f0 + flipped(f0, 2)) + (shifted(f1, 4) + crossed(f1))

    c2 = 4.0 * coarsen(inner(cond, k))
    d2 = OMEGA / (1.0 + 3.0 * c2)
    coarse = d2 * g2
    for _ in range(3):
        prior = shifted(coarse, 4)
        coarse = coarse + d2 * (g2 + prior - applied(framed(coarse, 1), c2, COARSE))

    e1, b1 = inner(d1, k), inner(g1, 2)
    middle = inner(rest1) + e1 * shifted(inner(m1, 2), 2) + refine(coarse)
    for _ in range(2):
        prior = shifted(middle, 2)
        middle = middle + e1 * (b1 + prior - applied(framed(middle, 1), c8))

    e0, c0, b0 = inner(d0, k), inner(cond, k), inner(g, k)
    even2 = inner(rest[0], 3) + e0 * (e0 * prior_odd)
    state = jnp.stack([even2, inner(odd2, 3)]) + middle

    def residual(v):
        prior = shifted(v[1], 2)
        before = jnp.stack([prior, v[0]])
        return b0 + before - applied(framed(v, 1, 1), c0)

    for _ in range(2):
        state = state + e0 * residual(state)
    last = residual(state)

    def whole(v):
        part = jnp.where(low, v[:, :, :HALF], v[:, :, ROWS - HALF :])
        keep, give = jnp.where(low, part[0], part[1]), jnp.where(low, part[1], part[0])
        other = flipped(give, 1)
        return jnp.concatenate(
            [jnp.where(low, keep, other), jnp.where(low, other, keep)], axis=1
        )

    return whole(state)[None], whole(last)[None]


def solution(mesh):
    return jax.shard_map(
        body,
        mesh=mesh,
        in_specs=(P("tm", "space", None, None), P("space", None, None)),
        out_specs=(P("tm", "space", None, None), P("tm", "space", None, None)),
        check_vma=False,
    )
```

```python
import jax
import jax.numpy as jnp
from jax import lax
from jax.sharding import PartitionSpec as P

OMEGA = 0.8
FINE = (1.0, 1.0, 1.0)
COARSE = (0.25, 0.25, 1.0)
HALF = 64
ROWS = 80
NARROW = 72


def shifted(value, by):
    peers = lax.axis_size("tm")
    return lax.ppermute(value, "tm", [(i, i + by) for i in range(peers) if 0 <= i + by < peers])


def flipped(value, mask):
    peers = lax.axis_size("tm")
    return lax.ppermute(value, "tm", [(i, i ^ mask) for i in range(peers)])


def exchanged(upward, downward):
    peers = lax.axis_size("space")
    up = [(i, i + 1) for i in range(peers - 1)]
    below = lax.ppermute(upward, "space", up)
    above = lax.ppermute(downward, "space", [(j, i) for i, j in up])
    return below, above


def framed(value, width, dim=0):
    length = value.shape[dim]
    before, after = exchanged(
        lax.slice_in_dim(value, length - width, length, axis=dim),
        lax.slice_in_dim(value, 0, width, axis=dim),
    )
    return jnp.concatenate([before, value, after], axis=dim)


def stencil(v, weights=FINE):
    a, b, d = weights
    m = v[..., 1:-1, :, :]
    lead = [(0, 0)] * (v.ndim - 2)
    px = jnp.pad(m, lead + [(1, 1), (0, 0)])
    py = jnp.pad(m, lead + [(0, 0), (1, 1)])
    return (
        2.0 * (a + b + d) * m
        - a * (v[..., 2:, :, :] + v[..., :-2, :, :])
        - b * (px[..., 2:, :] + px[..., :-2, :])
        - d * (py[..., 2:] + py[..., :-2])
    )


def inner(v, n=1):
    return v[..., n:-n, :, :]


def applied(v, c, weights=FINE):
    return inner(v) + c * stencil(v, weights)


def pair_matrix(rows):
    i = lax.broadcasted_iota(jnp.int32, (rows // 2, rows), 0)
    j = lax.broadcasted_iota(jnp.int32, (rows // 2, rows), 1)
    return (j // 2 == i).astype(jnp.float32)


def coarsen(v):
    z = v[..., 0::2, :, :] + v[..., 1::2, :, :]
    rows = z.shape[-2]
    return 0.25 * jnp.einsum(
        "ij,...jy->...iy", pair_matrix(rows), z, precision=lax.Precision.HIGHEST
    )


def refine(v):
    rows = v.shape[-2] * 2
    wide = jnp.einsum(
        "ij,...iy->...jy", pair_matrix(rows), v, precision=lax.Precision.HIGHEST
    )
    return jnp.repeat(wide, 2, axis=-3)


def body(source, conductivity):
    me = lax.axis_index("tm")
    odd_chip = (me // 2) % 2 == 1
    low = me % 2 == 0
    planes, rows, _ = conductivity.shape

    def window(v, keep):
        return jnp.where(keep, v[:, :ROWS], v[:, rows - ROWS :])

    def narrow(v):
        return jnp.where(low, v[..., :NARROW, :], v[..., ROWS - NARROW :, :])

    mine = window(source[0], low)
    got = flipped(window(source[0], ~low), 1)
    even, odd = jnp.where(low, mine, got), jnp.where(low, got, mine)
    prior_odd = shifted(odd, 2)
    bundle = framed(jnp.stack([even, odd, window(conductivity, low)]), 2, 1)
    bundle, prior_odd = lax.optimization_barrier((bundle, prior_odd))
    g, cond = bundle[:2], bundle[2]
    d0 = OMEGA / (1.0 + 6.0 * cond)
    d1 = OMEGA / (1.0 + 12.0 * cond)

    c10, c8 = inner(cond, 1), inner(cond, 2)
    u1 = d0 * g
    rest = inner(u1) + inner(d0) * (inner(g) - applied(u1, c10))
    hop = inner(d0) * inner(u1)
    odd2 = rest[1] + hop[0]
    w = inner(odd2) - c8 * stencil(hop[1])
    local = inner(g[0] + g[1], 2) + inner(rest[0]) - applied(rest[0] + odd2, c8)
    g1 = local + shifted(w, 2)

    def spill(v, n):
        return jnp.pad(v, ((n, n), (0, 0), (0, 0)))

    m1 = inner(d1, 2) * g1
    rest1 = spill(m1, 1) + inner(d1) * (spill(g1, 1) - applied(spill(m1, 2), 2.0 * c10))
    hop1 = inner(d1, 2) * m1
    own = spill(g1, 2) - applied(spill(rest1, 2), 2.0 * cond)
    nxt = spill(rest1, 1) - applied(spill(hop1, 3), 2.0 * cond)
    carry = spill(hop1, 2)
    pair = coarsen(
        jnp.stack([own + jnp.where(odd_chip, 0.0, nxt), carry + jnp.where(odd_chip, nxt, 0.0)])
    )
    pair = pair + flipped(pair, 2)

    c2 = 4.0 * coarsen(inner(cond, 2))
    split = g1.reshape(planes, 2, ROWS // 2, g1.shape[-1])
    below, above = exchanged(
        jnp.concatenate([pair[0, -5:], pair[1, -5:], c2[-3:], split[-1]]),
        jnp.concatenate([pair[0, :5], pair[1, :5], c2[:3], split[0]]),
    )

    def joined(part, lower, upper):
        first = part[1:2] + lower[4:5]
        last = part[-2:-1] + upper[0:1]
        before = jnp.concatenate([lower[1:3], lower[3:4] + part[0:1]])
        after = jnp.concatenate([upper[1:2] + part[-1:], upper[2:4]])
        return jnp.concatenate([before, first, part[2:-2], last, after])

    right = [
        joined(pair[i], below[5 * i : 5 * i + 5], above[5 * i : 5 * i + 5]) for i in range(2)
    ]
    c2 = jnp.concatenate([below[10:13], c2, above[10:13]])
    g1_wide = jnp.concatenate(
        [below[13:15].reshape(1, ROWS, -1), g1, above[13:15].reshape(1, ROWS, -1)]
    )
    d2 = OMEGA / (1.0 + 3.0 * c2)
    base = [d2 * v for v in right]
    share = list(base)
    for _ in range(3):
        c2 = inner(c2)
        d2 = inner(d2)
        base = [inner(v) for v in base]
        kept = [inner(v) - d2 * applied(v, c2, COARSE) for v in share]
        moved = [d2 * inner(v) for v in share]
        share = [
            sum(
                ([kept[j]] if j < len(kept) else [])
                + ([moved[j - 1]] if j else [])
                + ([base[j]] if j < 2 else [])
            )
            for j in range(len(kept) + 1)
        ]
    coarse = share[0]
    arrived = [shifted(share[j], 4 * j) for j in range(1, 5)]
    coarse = coarse + (arrived[0] + arrived[1]) + (arrived[2] + arrived[3])

    e1, b1, cc = narrow(inner(d1, 2)), narrow(g1), narrow(2.0 * c8)
    m1_wide = inner(d1) * g1_wide
    rest1 = m1 + inner(d1, 2) * (g1 - applied(m1_wide, 2.0 * c8))
    middle = narrow(rest1 + inner(d1, 2) * shifted(m1, 2) + refine(coarse))
    for _ in range(2):
        prior = shifted(middle, 2)
        middle = middle + e1 * (b1 + prior - applied(framed(middle, 1), cc))

    def half(v):
        return jnp.where(low, v[..., :HALF, :], v[..., v.shape[-2] - HALF :, :])

    e0 = half(inner(d0, 2))
    pre = [half(inner(rest[0])) + e0 * (e0 * half(prior_odd)), half(inner(odd2))]
    top = half(middle)
    keep = jnp.where(low, pre[0], pre[1]) + top
    other = flipped(jnp.where(low, pre[1], pre[0]) + top, 1)
    state = jnp.concatenate([jnp.where(low, keep, other), jnp.where(low, other, keep)], axis=1)
    b0 = source[0]
    d0 = OMEGA / (1.0 + 6.0 * conductivity)
    for _ in range(2):
        prior = shifted(state, 1)
        state = state + d0 * (b0 + prior - applied(framed(state, 1), conductivity))
    prior = shifted(state, 1)
    last = b0 + prior - applied(framed(state, 1), conductivity)
    return state[None], last[None]


def solution(mesh):
    return jax.shard_map(
        body,
        mesh=mesh,
        in_specs=(P("tm", "space", None, None), P("space", None, None)),
        out_specs=(P("tm", "space", None, None), P("tm", "space", None, None)),
        check_vma=False,
    )
```

```python
import jax
import jax.numpy as jnp
from jax import lax
from jax.sharding import PartitionSpec as P

OMEGA = 0.8
FINE = (1.0, 1.0, 1.0)
COARSE = (0.25, 0.25, 1.0)
HALF = 64
ROWS = 80
NARROW = 72


def shifted(value, by):
    peers = lax.axis_size("tm")
    return lax.ppermute(value, "tm", [(i, i + by) for i in range(peers) if 0 <= i + by < peers])


def flipped(value, mask):
    peers = lax.axis_size("tm")
    return lax.ppermute(value, "tm", [(i, i ^ mask) for i in range(peers)])


def exchanged(upward, downward):
    peers = lax.axis_size("space")
    up = [(i, i + 1) for i in range(peers - 1)]
    below = lax.ppermute(upward, "space", up)
    above = lax.ppermute(downward, "space", [(j, i) for i, j in up])
    return below, above


def slanted(upward, downward):
    times, peers = lax.axis_size("tm"), lax.axis_size("space")
    axes = ("tm", "space")
    steps = [(t * peers, (t + 2) * peers) for t in range(times - 2)]
    up = [(a + i, b + i + 1) for a, b in steps for i in range(peers - 1)]
    down = [(a + i + 1, b + i) for a, b in steps for i in range(peers - 1)]
    return lax.ppermute(upward, axes, up), lax.ppermute(downward, axes, down)


def framed(value, width, dim=0):
    length = value.shape[dim]
    before, after = exchanged(
        lax.slice_in_dim(value, length - width, length, axis=dim),
        lax.slice_in_dim(value, 0, width, axis=dim),
    )
    return jnp.concatenate([before, value, after], axis=dim)


def stencil(v, weights=FINE):
    a, b, d = weights
    m = v[..., 1:-1, :, :]
    lead = [(0, 0)] * (v.ndim - 2)
    px = jnp.pad(m, lead + [(1, 1), (0, 0)])
    py = jnp.pad(m, lead + [(0, 0), (1, 1)])
    return (
        2.0 * (a + b + d) * m
        - a * (v[..., 2:, :, :] + v[..., :-2, :, :])
        - b * (px[..., 2:, :] + px[..., :-2, :])
        - d * (py[..., 2:] + py[..., :-2])
    )


def inner(v, n=1):
    return v[..., n:-n, :, :]


def applied(v, c, weights=FINE):
    return inner(v) + c * stencil(v, weights)


def pair_matrix(rows):
    i = lax.broadcasted_iota(jnp.int32, (rows // 2, rows), 0)
    j = lax.broadcasted_iota(jnp.int32, (rows // 2, rows), 1)
    return (j // 2 == i).astype(jnp.float32)


def coarsen(v):
    z = v[..., 0::2, :, :] + v[..., 1::2, :, :]
    rows = z.shape[-2]
    return 0.25 * jnp.einsum(
        "ij,...jy->...iy", pair_matrix(rows), z, precision=lax.Precision.HIGHEST
    )


def refine(v):
    rows = v.shape[-2] * 2
    wide = jnp.einsum(
        "ij,...iy->...jy", pair_matrix(rows), v, precision=lax.Precision.HIGHEST
    )
    return jnp.repeat(wide, 2, axis=-3)


def body(source, conductivity):
    me = lax.axis_index("tm")
    odd_chip = (me // 2) % 2 == 1
    low = me % 2 == 0
    planes, rows, _ = conductivity.shape

    def window(v, keep):
        return jnp.where(keep, v[:, :ROWS], v[:, rows - ROWS :])

    def narrow(v):
        return jnp.where(low, v[..., :NARROW, :], v[..., ROWS - NARROW :, :])

    mine = window(source[0], low)
    got = flipped(window(source[0], ~low), 1)
    even, odd = jnp.where(low, mine, got), jnp.where(low, got, mine)
    bundle = framed(jnp.stack([even, odd, window(conductivity, low)]), 2, 1)
    g, cond = bundle[:2], bundle[2]
    d0 = OMEGA / (1.0 + 6.0 * cond)
    d1 = OMEGA / (1.0 + 12.0 * cond)

    c10, c8 = inner(cond, 1), inner(cond, 2)
    u1 = d0 * g
    rest = inner(u1) + inner(d0) * (inner(g) - applied(u1, c10))
    hop = inner(d0) * inner(u1)
    odd2 = rest[1] + hop[0]
    w = inner(odd2) - c8 * stencil(hop[1])
    local = inner(g[0] + g[1], 2) + inner(rest[0]) - applied(rest[0] + odd2, c8)
    g1 = local + shifted(w, 2)

    def spill(v, n):
        return jnp.pad(v, ((n, n), (0, 0), (0, 0)))

    m1 = inner(d1, 2) * g1
    rest1 = spill(m1, 1) + inner(d1) * (spill(g1, 1) - applied(spill(m1, 2), 2.0 * c10))
    hop1 = inner(d1, 2) * m1
    own = spill(g1, 2) - applied(spill(rest1, 2), 2.0 * cond)
    nxt = spill(rest1, 1) - applied(spill(hop1, 3), 2.0 * cond)
    carry = spill(hop1, 2)
    pair = coarsen(
        jnp.stack([own + jnp.where(odd_chip, 0.0, nxt), carry + jnp.where(odd_chip, nxt, 0.0)])
    )
    pair = pair + flipped(pair, 2)

    c2 = 4.0 * coarsen(inner(cond, 2))
    split = g1.reshape(planes, 2, ROWS // 2, g1.shape[-1])
    below, above = exchanged(
        jnp.concatenate([pair[0, -5:], pair[1, -5:], c2[-3:], split[-1]]),
        jnp.concatenate([pair[0, :5], pair[1, :5], c2[:3], split[0]]),
    )

    def joined(part, lower, upper):
        first = part[1:2] + lower[4:5]
        last = part[-2:-1] + upper[0:1]
        before = jnp.concatenate([lower[1:3], lower[3:4] + part[0:1]])
        after = jnp.concatenate([upper[1:2] + part[-1:], upper[2:4]])
        return jnp.concatenate([before, first, part[2:-2], last, after])

    right = [
        joined(pair[i], below[5 * i : 5 * i + 5], above[5 * i : 5 * i + 5]) for i in range(2)
    ]
    c2 = jnp.concatenate([below[10:13], c2, above[10:13]])
    g1_wide = jnp.concatenate(
        [below[13:15].reshape(1, ROWS, -1), g1, above[13:15].reshape(1, ROWS, -1)]
    )
    d2 = OMEGA / (1.0 + 3.0 * c2)
    base = [d2 * v for v in right]
    share = list(base)
    for _ in range(3):
        c2 = inner(c2)
        d2 = inner(d2)
        base = [inner(v) for v in base]
        kept = [inner(v) - d2 * applied(v, c2, COARSE) for v in share]
        moved = [d2 * inner(v) for v in share]
        share = [
            sum(
                ([kept[j]] if j < len(kept) else [])
                + ([moved[j - 1]] if j else [])
                + ([base[j]] if j < 2 else [])
            )
            for j in range(len(kept) + 1)
        ]
    coarse = share[0]
    arrived = [shifted(share[j], 4 * j) for j in range(1, 5)]
    coarse = coarse + (arrived[0] + arrived[1]) + (arrived[2] + arrived[3])

    e1, b1, cc = narrow(inner(d1, 2)), narrow(g1), narrow(2.0 * c8)
    m1_wide = inner(d1) * g1_wide
    rest1 = m1 + inner(d1, 2) * (g1 - applied(m1_wide, 2.0 * c8))
    middle = narrow(rest1 + inner(d1, 2) * shifted(m1, 2) + refine(coarse))
    for _ in range(2):
        prior = shifted(middle, 2)
        middle = middle + e1 * (b1 + prior - applied(framed(middle, 1), cc))

    g, d0, cond = narrow(g), narrow(d0), narrow(cond)
    e0 = inner(d0, 2)
    prior_odd = shifted(inner(g[1], 2), 2)
    pre = jnp.stack([narrow(inner(rest[0])) + e0 * (e0 * prior_odd), narrow(inner(odd2))])
    state = pre + middle
    sent = shifted(jnp.stack([state[1], e0 * (inner(g[1], 2) + state[0])]), 2)
    state = framed(state, 2, 1)
    lower, upper = slanted(state[1, -3:-2], state[1, 2:3])
    earlier = jnp.concatenate([lower, sent[0], upper])

    def swept(v, width):
        return inner(v) - inner(d0, width) * applied(v, inner(cond, width))

    before = jnp.stack([earlier, inner(state[0])])
    state = swept(state, 1) + inner(d0) * (inner(g) + before)
    earlier = swept(earlier, 2) + sent[1]
    before = jnp.stack([earlier, inner(state[0])])
    state = swept(state, 2) + e0 * (inner(g, 2) + before)

    half = jnp.where(low, state[:, :, :HALF], state[:, :, NARROW - HALF :])
    keep = jnp.where(low, half[0], half[1])
    other = flipped(jnp.where(low, half[1], half[0]), 1)
    state = jnp.concatenate([jnp.where(low, keep, other), jnp.where(low, other, keep)], axis=1)
    last = source[0] + shifted(state, 1) - applied(framed(state, 1), conductivity)
    return state[None], last[None]


def solution(mesh):
    return jax.shard_map(
        body,
        mesh=mesh,
        in_specs=(P("tm", "space", None, None), P("space", None, None)),
        out_specs=(P("tm", "space", None, None), P("tm", "space", None, None)),
        check_vma=False,
    )
```

```python
import jax
import jax.numpy as jnp
from jax import lax
from jax.sharding import PartitionSpec as P

OMEGA = 0.8
FINE = (1.0, 1.0, 1.0)
COARSE = (0.25, 0.25, 1.0)
HALF = 64
ROWS = 80
NARROW = 72


def shifted(value, by):
    peers = lax.axis_size("tm")
    return lax.ppermute(value, "tm", [(i, i + by) for i in range(peers) if 0 <= i + by < peers])


def flipped(value, mask):
    peers = lax.axis_size("tm")
    return lax.ppermute(value, "tm", [(i, i ^ mask) for i in range(peers)])


def exchanged(upward, downward):
    peers = lax.axis_size("space")
    up = [(i, i + 1) for i in range(peers - 1)]
    below = lax.ppermute(upward, "space", up)
    above = lax.ppermute(downward, "space", [(j, i) for i, j in up])
    return below, above


def framed(value, width, dim=0):
    length = value.shape[dim]
    before, after = exchanged(
        lax.slice_in_dim(value, length - width, length, axis=dim),
        lax.slice_in_dim(value, 0, width, axis=dim),
    )
    return jnp.concatenate([before, value, after], axis=dim)


def stencil(v, weights=FINE):
    a, b, d = weights
    m = v[..., 1:-1, :, :]
    lead = [(0, 0)] * (v.ndim - 2)
    px = jnp.pad(m, lead + [(1, 1), (0, 0)])
    py = jnp.pad(m, lead + [(0, 0), (1, 1)])
    return (
        2.0 * (a + b + d) * m
        - a * (v[..., 2:, :, :] + v[..., :-2, :, :])
        - b * (px[..., 2:, :] + px[..., :-2, :])
        - d * (py[..., 2:] + py[..., :-2])
    )


def inner(v, n=1):
    return v[..., n:-n, :, :]


def applied(v, c, weights=FINE):
    return inner(v) + c * stencil(v, weights)


def pair_matrix(rows):
    i = lax.broadcasted_iota(jnp.int32, (rows // 2, rows), 0)
    j = lax.broadcasted_iota(jnp.int32, (rows // 2, rows), 1)
    return (j // 2 == i).astype(jnp.float32)


def coarsen(v):
    z = v[..., 0::2, :, :] + v[..., 1::2, :, :]
    rows = z.shape[-2]
    return 0.25 * jnp.einsum(
        "ij,...jy->...iy", pair_matrix(rows), z, precision=lax.Precision.HIGHEST
    )


def refine(v):
    rows = v.shape[-2] * 2
    wide = jnp.einsum(
        "ij,...iy->...jy", pair_matrix(rows), v, precision=lax.Precision.HIGHEST
    )
    return jnp.repeat(wide, 2, axis=-3)


def body(source, conductivity):
    me = lax.axis_index("tm")
    odd_chip = (me // 2) % 2 == 1
    low = me % 2 == 0
    planes, rows, _ = conductivity.shape

    def window(v, keep):
        return jnp.where(keep, v[:, :ROWS], v[:, rows - ROWS :])

    def narrow(v):
        return jnp.where(low, v[..., :NARROW, :], v[..., ROWS - NARROW :, :])

    mine = window(source[0], low)
    got = flipped(window(source[0], ~low), 1)
    even, odd = jnp.where(low, mine, got), jnp.where(low, got, mine)
    bundle = framed(jnp.stack([even, odd, window(conductivity, low)]), 3, 1)
    g, cond = bundle[:2], bundle[2]
    d0 = OMEGA / (1.0 + 6.0 * cond)
    d1 = OMEGA / (1.0 + 12.0 * cond)

    c12, c10, c8 = inner(cond, 1), inner(cond, 2), inner(cond, 3)
    u1 = d0 * g
    rest = inner(u1) + inner(d0) * (inner(g) - applied(u1, c12))
    hop = inner(d0) * inner(u1)
    odd2 = rest[1] + hop[0]
    w = inner(odd2) - c10 * stencil(hop[1])
    local = inner(g[0] + g[1], 2) + inner(rest[0]) - applied(rest[0] + odd2, c10)
    before_w = shifted(narrow(w), 2)

    def spill(v, n):
        return jnp.pad(v, ((0, 0), (n, n), (0, 0), (0, 0)))

    part = jnp.stack([inner(local), inner(w)])
    first = inner(d1, 3) * part
    swept1 = spill(first, 1) + inner(d1, 2) * (
        spill(part, 1) - applied(spill(first, 2), 2.0 * c10)
    )
    hop1 = inner(d1, 3) * first
    own = spill(part, 2) - applied(spill(swept1, 2), 2.0 * c12)
    nxt = spill(swept1, 1) - applied(spill(hop1, 3), 2.0 * c12)
    carry = spill(hop1, 2)
    share = coarsen(
        jnp.stack(
            [
                own[0] + jnp.where(odd_chip, 0.0, nxt[0] + own[1]),
                carry[0]
                + nxt[1]
                + jnp.where(odd_chip, nxt[0] + own[1], carry[1]),
                jnp.where(odd_chip, carry[1], 0.0),
            ]
        )
    )

    c2 = 4.0 * coarsen(c8)
    below, above = exchanged(
        jnp.concatenate([share[0, -5:], share[1, -5:], share[2, -5:], c2[-3:]]),
        jnp.concatenate([share[0, :5], share[1, :5], share[2, :5], c2[:3]]),
    )

    def joined(v, lower, upper):
        head, tail = v[1:2] + lower[4:5], v[-2:-1] + upper[0:1]
        before = jnp.concatenate([lower[1:3], lower[3:4] + v[0:1]])
        after = jnp.concatenate([upper[1:2] + v[-1:], upper[2:4]])
        return jnp.concatenate([before, head, v[2:-2], tail, after])

    right = [
        joined(share[i], below[5 * i : 5 * i + 5], above[5 * i : 5 * i + 5]) for i in range(3)
    ]
    c2 = jnp.concatenate([below[15:], c2, above[15:]])
    d2 = OMEGA / (1.0 + 3.0 * c2)
    base = [d2 * v for v in right]
    terms = list(base)
    for _ in range(3):
        c2, d2 = inner(c2), inner(d2)
        base = [inner(v) for v in base]
        kept = [inner(v) - d2 * applied(v, c2, COARSE) for v in terms]
        moved = [d2 * inner(v) for v in terms]
        count = len(terms)
        terms = [
            sum(
                ([kept[j]] if j < count else [])
                + ([moved[j - 1]] if j else [])
                + ([base[j]] if j < 3 else [])
            )
            for j in range(count + 1)
        ]
    coarse = terms[0]
    for j in range(1, 6):
        coarse = coarse + shifted(terms[j], 4 * j)
    coarse = coarse + flipped(coarse, 2)

    g, cond, d0, d1 = narrow(g), narrow(cond), narrow(d0), narrow(d1)
    g1 = narrow(local) + before_w
    m1 = inner(d1, 2) * g1
    prior = shifted(jnp.stack([inner(m1), inner(g[1], 3)]), 2)
    e1, b1, cc = inner(d1, 3), inner(g1), 2.0 * inner(cond, 3)
    rest1 = inner(m1) + e1 * (b1 - applied(m1, cc))
    middle = rest1 + e1 * prior[0] + narrow(refine(coarse))
    for _ in range(2):
        earlier = shifted(middle, 2)
        middle = middle + e1 * (b1 + earlier - applied(framed(middle, 1), cc))

    g, cond, d0 = inner(g), inner(cond), inner(d0)
    e0 = inner(d0, 2)
    pre = jnp.stack(
        [narrow(inner(rest[0], 2)) + e0 * (e0 * prior[1]), narrow(inner(odd2, 2))]
    )
    state = pre + middle
    sent = shifted(jnp.stack([state[1], e0 * (inner(g[1], 2) + state[0])]), 2)
    state = framed(state, 2, 1)
    ghost = jnp.pad(sent[0], ((1, 1), (0, 0), (0, 0)))

    def swept(v, width):
        return inner(v) - inner(d0, width) * applied(v, inner(cond, width))

    before = jnp.stack([ghost, inner(state[0])])
    state = swept(state, 1) + inner(d0) * (inner(g) + before)
    before = jnp.stack([swept(ghost, 2) + sent[1], inner(state[0])])
    state = swept(state, 2) + e0 * (inner(g, 2) + before)

    def half(v):
        return jnp.where(low, v[..., :HALF, :], v[..., NARROW - HALF :, :])

    both = half(state)
    faces = half(
        jnp.concatenate([sent[0][:1], sent[0][-1:], cond[1:2], cond[-2:-1]])
    )
    keep = jnp.concatenate([jnp.where(low, both[0], both[1]), faces])
    other = flipped(jnp.concatenate([jnp.where(low, both[1], both[0]), faces]), 1)
    full = jnp.concatenate([jnp.where(low, keep, other), jnp.where(low, other, keep)], axis=1)
    state, lead, beyond = full[:planes], full[planes : planes + 2], full[planes + 2 :]
    earlier = shifted(state, 1)
    below, above = exchanged(
        jnp.concatenate([state[-1:], lead[1:]]), jnp.concatenate([state[:1], lead[:1]])
    )
    edge = jnp.concatenate([conductivity[:1], conductivity[-1:]])
    de, db = OMEGA / (1.0 + 6.0 * edge), OMEGA / (1.0 + 6.0 * beyond)
    inside = de * edge * (de + db) * jnp.concatenate([below[1:], above[1:]])
    outside = db * beyond * (de + db) * lead
    outside = jnp.where(low, outside, 0.0)

    def mended(v, keep):
        fix = jnp.where(keep, inside, 0.0)
        return jnp.concatenate([v[:1] + fix[:1], v[1:-1], v[-1:] + fix[1:]])

    state, earlier = mended(state, low), mended(earlier, ~low)
    wide = jnp.concatenate([below[:1] + outside[:1], state, above[:1] + outside[1:]])
    last = source[0] + earlier - applied(wide, conductivity)
    return state[None], last[None]


def solution(mesh):
    return jax.shard_map(
        body,
        mesh=mesh,
        in_specs=(P("tm", "space", None, None), P("space", None, None)),
        out_specs=(P("tm", "space", None, None), P("tm", "space", None, None)),
        check_vma=False,
    )
```

```python
import jax
import jax.numpy as jnp
from jax import lax
from jax.sharding import PartitionSpec as P

OMEGA = 0.8
FINE = (1.0, 1.0, 1.0)
COARSE = (0.25, 0.25, 1.0)
HALF = 64
ROWS = 80
NARROW = 72


def shifted(value, by):
    peers = lax.axis_size("tm")
    return lax.ppermute(value, "tm", [(i, i + by) for i in range(peers) if 0 <= i + by < peers])


def flipped(value, mask):
    peers = lax.axis_size("tm")
    return lax.ppermute(value, "tm", [(i, i ^ mask) for i in range(peers)])


def exchanged(upward, downward):
    peers = lax.axis_size("space")
    up = [(i, i + 1) for i in range(peers - 1)]
    below = lax.ppermute(upward, "space", up)
    above = lax.ppermute(downward, "space", [(j, i) for i, j in up])
    return below, above


def slanted(upward, downward):
    times, peers = lax.axis_size("tm"), lax.axis_size("space")
    axes = ("tm", "space")
    steps = [(t * peers, (t + 2) * peers) for t in range(times - 2)]
    up = [(a + i, b + i + 1) for a, b in steps for i in range(peers - 1)]
    down = [(a + i + 1, b + i) for a, b in steps for i in range(peers - 1)]
    return lax.ppermute(upward, axes, up), lax.ppermute(downward, axes, down)


def framed(value, width, dim=0):
    length = value.shape[dim]
    before, after = exchanged(
        lax.slice_in_dim(value, length - width, length, axis=dim),
        lax.slice_in_dim(value, 0, width, axis=dim),
    )
    return jnp.concatenate([before, value, after], axis=dim)


def stencil(v, weights=FINE):
    a, b, d = weights
    m = v[..., 1:-1, :, :]
    lead = [(0, 0)] * (v.ndim - 2)
    px = jnp.pad(m, lead + [(1, 1), (0, 0)])
    py = jnp.pad(m, lead + [(0, 0), (1, 1)])
    return (
        2.0 * (a + b + d) * m
        - a * (v[..., 2:, :, :] + v[..., :-2, :, :])
        - b * (px[..., 2:, :] + px[..., :-2, :])
        - d * (py[..., 2:] + py[..., :-2])
    )


def inner(v, n=1):
    return v[..., n:-n, :, :]


def applied(v, c, weights=FINE):
    return inner(v) + c * stencil(v, weights)


def pair_matrix(rows):
    i = lax.broadcasted_iota(jnp.int32, (rows // 2, rows), 0)
    j = lax.broadcasted_iota(jnp.int32, (rows // 2, rows), 1)
    return (j // 2 == i).astype(jnp.float32)


def coarsen(v):
    z = v[..., 0::2, :, :] + v[..., 1::2, :, :]
    rows = z.shape[-2]
    return 0.25 * jnp.einsum(
        "ij,...jy->...iy", pair_matrix(rows), z, precision=lax.Precision.HIGHEST
    )


def refine(v):
    rows = v.shape[-2] * 2
    wide = jnp.einsum(
        "ij,...iy->...jy", pair_matrix(rows), v, precision=lax.Precision.HIGHEST
    )
    return jnp.repeat(wide, 2, axis=-3)


def body(source, conductivity):
    me = lax.axis_index("tm")
    odd_chip = (me // 2) % 2 == 1
    low = me % 2 == 0
    planes, rows, _ = conductivity.shape

    def window(v, keep):
        return jnp.where(keep, v[:, :ROWS], v[:, rows - ROWS :])

    def narrow(v):
        return jnp.where(low, v[..., :NARROW, :], v[..., ROWS - NARROW :, :])

    mine = window(source[0], low)
    got = flipped(window(source[0], ~low), 1)
    even, odd = jnp.where(low, mine, got), jnp.where(low, got, mine)
    bundle = framed(jnp.stack([even, odd, window(conductivity, low)]), 2, 1)
    g, cond = bundle[:2], bundle[2]
    d0 = OMEGA / (1.0 + 6.0 * cond)
    d1 = OMEGA / (1.0 + 12.0 * cond)

    def spill(v, n):
        return jnp.pad(v, ((n, n), (0, 0), (0, 0)))

    cw = window(conductivity, low)
    dw = OMEGA / (1.0 + 6.0 * cw)
    u1 = dw * odd
    w = u1 + dw * (odd - applied(spill(u1, 1), cw)) + dw * (dw * even)
    w = w - cw * stencil(spill(dw * u1, 1))
    before_w = shifted(w, 2)
    lower, upper = slanted(odd[-1:], odd[:1])

    c10, c8 = inner(cond, 1), inner(cond, 2)
    u1 = d0 * g
    rest = inner(u1) + inner(d0) * (inner(g) - applied(u1, c10))
    odd2 = rest[1] + inner(d0[None] * u1)[0]
    local = inner(g[0] + g[1], 2) + inner(rest[0]) - applied(rest[0] + odd2, c8)
    lower = c8[:1] * (d0[2:3] + d0[1:2]) * (d0[1:2] * lower)
    upper = c8[-1:] * (d0[-3:-2] + d0[-2:-1]) * (d0[-2:-1] * upper)
    g1 = local + jnp.concatenate([before_w[:1] + lower, before_w[1:-1], before_w[-1:] + upper])

    m1 = inner(d1, 2) * g1
    rest1 = spill(m1, 1) + inner(d1) * (spill(g1, 1) - applied(spill(m1, 2), 2.0 * c10))
    hop1 = inner(d1, 2) * m1
    own = spill(g1, 2) - applied(spill(rest1, 2), 2.0 * cond)
    nxt = spill(rest1, 1) - applied(spill(hop1, 3), 2.0 * cond)
    carry = spill(hop1, 2)
    share = coarsen(
        jnp.stack([own + jnp.where(odd_chip, 0.0, nxt), carry + jnp.where(odd_chip, nxt, 0.0)])
    )

    c2 = 4.0 * coarsen(c8)
    split = g1.reshape(planes, 2, ROWS // 2, g1.shape[-1])
    below, above = exchanged(
        jnp.concatenate([share[0, -5:], share[1, -5:], c2[-3:], split[-1]]),
        jnp.concatenate([share[0, :5], share[1, :5], c2[:3], split[0]]),
    )

    def joined(v, lower, upper):
        head, tail = v[1:2] + lower[4:5], v[-2:-1] + upper[0:1]
        before = jnp.concatenate([lower[1:3], lower[3:4] + v[0:1]])
        after = jnp.concatenate([upper[1:2] + v[-1:], upper[2:4]])
        return jnp.concatenate([before, head, v[2:-2], tail, after])

    right = [
        joined(share[i], below[5 * i : 5 * i + 5], above[5 * i : 5 * i + 5]) for i in range(2)
    ]
    c2 = jnp.concatenate([below[10:13], c2, above[10:13]])
    g1_wide = jnp.concatenate(
        [below[13:].reshape(1, ROWS, -1), g1, above[13:].reshape(1, ROWS, -1)]
    )
    d2 = OMEGA / (1.0 + 3.0 * c2)
    base = [d2 * v for v in right]
    terms = list(base)
    for _ in range(3):
        c2, d2 = inner(c2), inner(d2)
        base = [inner(v) for v in base]
        kept = [inner(v) - d2 * applied(v, c2, COARSE) for v in terms]
        moved = [d2 * inner(v) for v in terms]
        count = len(terms)
        terms = [
            sum(
                ([kept[j]] if j < count else [])
                + ([moved[j - 1]] if j else [])
                + ([base[j]] if j < 2 else [])
            )
            for j in range(count + 1)
        ]
    arrived = [shifted(terms[j], 4 * j) for j in range(1, 5)]
    coarse = terms[0] + (arrived[0] + arrived[1]) + (arrived[2] + arrived[3])
    coarse = coarse + flipped(coarse, 2)

    prior_m1, prior_odd = shifted(jnp.stack([narrow(m1), narrow(odd)]), 2)
    g, cond, d0, d1 = narrow(g), narrow(cond), narrow(d0), narrow(d1)
    g1 = narrow(g1_wide)
    m1 = inner(d1) * g1
    e1, b1, cc = inner(d1, 2), inner(g1), 2.0 * inner(cond, 2)
    rest1 = inner(m1) + e1 * (b1 - applied(m1, cc))
    middle = rest1 + e1 * prior_m1 + narrow(refine(coarse))
    for _ in range(2):
        earlier = shifted(middle, 2)
        middle = middle + e1 * (b1 + earlier - applied(framed(middle, 1), cc))

    e0 = inner(d0, 2)
    pre = jnp.stack([narrow(inner(rest[0])) + e0 * (e0 * prior_odd), narrow(inner(odd2))])
    state = pre + middle
    sent = shifted(jnp.stack([state[1], e0 * (inner(g[1], 2) + state[0])]), 2)
    state = framed(state, 2, 1)
    ghost = jnp.pad(sent[0], ((1, 1), (0, 0), (0, 0)))

    def swept(v, width):
        return inner(v) - inner(d0, width) * applied(v, inner(cond, width))

    before = jnp.stack([ghost, inner(state[0])])
    state = swept(state, 1) + inner(d0) * (inner(g) + before)
    before = jnp.stack([swept(ghost, 2) + sent[1], inner(state[0])])
    state = swept(state, 2) + e0 * (inner(g, 2) + before)

    def half(v):
        return jnp.where(low, v[..., :HALF, :], v[..., NARROW - HALF :, :])

    both = half(state)
    faces = half(
        jnp.concatenate([sent[0][:1], sent[0][-1:], cond[1:2], cond[-2:-1]])
    )
    keep = jnp.concatenate([jnp.where(low, both[0], both[1]), faces])
    other = flipped(jnp.concatenate([jnp.where(low, both[1], both[0]), faces]), 1)
    full = jnp.concatenate([jnp.where(low, keep, other), jnp.where(low, other, keep)], axis=1)
    state, lead, beyond = full[:planes], full[planes : planes + 2], full[planes + 2 :]
    earlier = shifted(state, 1)
    below, above = exchanged(
        jnp.concatenate([state[-1:], lead[1:]]), jnp.concatenate([state[:1], lead[:1]])
    )
    below, above, earlier = lax.optimization_barrier((below, above, earlier))
    edge = jnp.concatenate([conductivity[:1], conductivity[-1:]])
    de, db = OMEGA / (1.0 + 6.0 * edge), OMEGA / (1.0 + 6.0 * beyond)
    inside = de * edge * (de + db) * jnp.concatenate([below[1:], above[1:]])
    outside = db * beyond * (de + db) * lead
    outside = jnp.where(low, outside, 0.0)

    def mended(v, keep):
        fix = jnp.where(keep, inside, 0.0)
        return jnp.concatenate([v[:1] + fix[:1], v[1:-1], v[-1:] + fix[1:]])

    state, earlier = mended(state, low), mended(earlier, ~low)
    wide = jnp.concatenate([below[:1] + outside[:1], state, above[:1] + outside[1:]])
    last = source[0] + earlier - applied(wide, conductivity)
    return state[None], last[None]


def solution(mesh):
    return jax.shard_map(
        body,
        mesh=mesh,
        in_specs=(P("tm", "space", None, None), P("space", None, None)),
        out_specs=(P("tm", "space", None, None), P("tm", "space", None, None)),
        check_vma=False,
    )
```

```python
import jax
import jax.numpy as jnp
import numpy as np
from jax import lax
from jax.sharding import PartitionSpec as P

OMEGA = 0.8
FINE = (1.0, 1.0, 1.0)
COARSE = (0.25, 0.25, 1.0)
HALF = 64
ROWS = 80
NARROW = 72


def shifted(value, by):
    peers = lax.axis_size("tm")
    return lax.ppermute(value, "tm", [(i, i + by) for i in range(peers) if 0 <= i + by < peers])


def flipped(value, mask):
    peers = lax.axis_size("tm")
    return lax.ppermute(value, "tm", [(i, i ^ mask) for i in range(peers)])


def exchanged(upward, downward):
    peers = lax.axis_size("space")
    up = [(i, i + 1) for i in range(peers - 1)]
    below = lax.ppermute(upward, "space", up)
    above = lax.ppermute(downward, "space", [(j, i) for i, j in up])
    return below, above


def slanted(upward, downward):
    times, peers = lax.axis_size("tm"), lax.axis_size("space")
    axes = ("tm", "space")
    steps = [(t * peers, (t + 2) * peers) for t in range(times - 2)]
    up = [(a + i, b + i + 1) for a, b in steps for i in range(peers - 1)]
    down = [(a + i + 1, b + i) for a, b in steps for i in range(peers - 1)]
    return lax.ppermute(upward, axes, up), lax.ppermute(downward, axes, down)


def framed(value, width, dim=0):
    length = value.shape[dim]
    before, after = exchanged(
        lax.slice_in_dim(value, length - width, length, axis=dim),
        lax.slice_in_dim(value, 0, width, axis=dim),
    )
    return jnp.concatenate([before, value, after], axis=dim)


def stencil(v, weights=FINE):
    a, b, d = weights
    m = v[..., 1:-1, :, :]
    lead = [(0, 0)] * (v.ndim - 2)
    px = jnp.pad(m, lead + [(1, 1), (0, 0)])
    py = jnp.pad(m, lead + [(0, 0), (1, 1)])
    return (
        2.0 * (a + b + d) * m
        - a * (v[..., 2:, :, :] + v[..., :-2, :, :])
        - b * (px[..., 2:, :] + px[..., :-2, :])
        - d * (py[..., 2:] + py[..., :-2])
    )


def inner(v, n=1):
    return v[..., n:-n, :, :]


def applied(v, c, weights=FINE):
    return inner(v) + c * stencil(v, weights)


def pair_matrix(rows):
    return np.repeat(np.eye(rows // 2, dtype=np.float32), 2, axis=1)


def coarsen(v):
    z = v[..., 0::2, :, :] + v[..., 1::2, :, :]
    rows = z.shape[-2]
    return 0.25 * jnp.einsum(
        "ij,...jy->...iy", pair_matrix(rows), z, precision=lax.Precision.HIGHEST
    )


def refine(v):
    rows = v.shape[-2] * 2
    wide = jnp.einsum(
        "ij,...iy->...jy", pair_matrix(rows), v, precision=lax.Precision.HIGHEST
    )
    return jnp.repeat(wide, 2, axis=-3)


def body(source, conductivity):
    me = lax.axis_index("tm")
    odd_chip = (me // 2) % 2 == 1
    low = me % 2 == 0
    planes, rows, _ = conductivity.shape

    def window(v, keep):
        return jnp.where(keep, v[:, :ROWS], v[:, rows - ROWS :])

    def narrow(v):
        return jnp.where(low, v[..., :NARROW, :], v[..., ROWS - NARROW :, :])

    mine = window(source[0], low)
    got = flipped(window(source[0], ~low), 1)
    even, odd = jnp.where(low, mine, got), jnp.where(low, got, mine)

    def spill(v, n):
        return jnp.pad(v, ((n, n), (0, 0), (0, 0)))

    cw = window(conductivity, low)
    dw = OMEGA / (1.0 + 6.0 * cw)
    u1 = dw * odd
    w = u1 + dw * (odd - applied(spill(u1, 1), cw)) + dw * (dw * even)
    w = w - cw * stencil(spill(dw * u1, 1))
    before_w = shifted(w, 2)
    slab = jnp.stack([even, odd, cw]) + 0.0 * w
    lower, upper = slanted(odd[-1:], odd[:1])

    bundle = framed(slab, 2, 1)
    bundle = jnp.concatenate([bundle[:, :2] + 0.0 * before_w[:2], bundle[:, 2:]], axis=1)
    g, cond = bundle[:2], bundle[2]
    d0 = OMEGA / (1.0 + 6.0 * cond)
    d1 = OMEGA / (1.0 + 12.0 * cond)

    c10, c8 = inner(cond, 1), inner(cond, 2)
    u1 = d0 * g
    rest = inner(u1) + inner(d0) * (inner(g) - applied(u1, c10))
    odd2 = rest[1] + inner(d0[None] * u1)[0]
    local = inner(g[0] + g[1], 2) + inner(rest[0]) - applied(rest[0] + odd2, c8)
    lower = c8[:1] * (d0[2:3] + d0[1:2]) * (d0[1:2] * lower)
    upper = c8[-1:] * (d0[-3:-2] + d0[-2:-1]) * (d0[-2:-1] * upper)
    g1 = local + jnp.concatenate([before_w[:1] + lower, before_w[1:-1], before_w[-1:] + upper])

    m1 = inner(d1, 2) * g1
    rest1 = spill(m1, 1) + inner(d1) * (spill(g1, 1) - applied(spill(m1, 2), 2.0 * c10))
    hop1 = inner(d1, 2) * m1
    own = spill(g1, 2) - applied(spill(rest1, 2), 2.0 * cond)
    nxt = spill(rest1, 1) - applied(spill(hop1, 3), 2.0 * cond)
    carry = spill(hop1, 2)
    share = coarsen(
        jnp.stack([own + jnp.where(odd_chip, 0.0, nxt), carry + jnp.where(odd_chip, nxt, 0.0)])
    )

    c2 = 4.0 * coarsen(c8)
    split = g1.reshape(planes, 2, ROWS // 2, g1.shape[-1])
    below, above = exchanged(
        jnp.concatenate([share[0, -5:], share[1, -5:], c2[-3:], split[-1]]),
        jnp.concatenate([share[0, :5], share[1, :5], c2[:3], split[0]]),
    )

    def joined(v, lower, upper):
        head, tail = v[1:2] + lower[4:5], v[-2:-1] + upper[0:1]
        before = jnp.concatenate([lower[1:3], lower[3:4] + v[0:1]])
        after = jnp.concatenate([upper[1:2] + v[-1:], upper[2:4]])
        return jnp.concatenate([before, head, v[2:-2], tail, after])

    right = [
        joined(share[i], below[5 * i : 5 * i + 5], above[5 * i : 5 * i + 5]) for i in range(2)
    ]
    c2 = jnp.concatenate([below[10:13], c2, above[10:13]])
    g1_wide = jnp.concatenate(
        [below[13:].reshape(1, ROWS, -1), g1, above[13:].reshape(1, ROWS, -1)]
    )
    d2 = OMEGA / (1.0 + 3.0 * c2)
    base = [d2 * v for v in right]
    terms = list(base)
    for _ in range(3):
        c2, d2 = inner(c2), inner(d2)
        base = [inner(v) for v in base]
        kept = [inner(v) - d2 * applied(v, c2, COARSE) for v in terms]
        moved = [d2 * inner(v) for v in terms]
        count = len(terms)
        terms = [
            sum(
                ([kept[j]] if j < count else [])
                + ([moved[j - 1]] if j else [])
                + ([base[j]] if j < 2 else [])
            )
            for j in range(count + 1)
        ]
    arrived = [shifted(terms[j], 4 * j) for j in range(1, 5)]
    coarse = terms[0] + (arrived[0] + arrived[1]) + (arrived[2] + arrived[3])
    coarse = coarse + flipped(coarse, 2)

    prior_m1, prior_odd = shifted(jnp.stack([narrow(m1), narrow(odd)]), 2)
    g, cond, d0, d1 = narrow(g), narrow(cond), narrow(d0), narrow(d1)
    g1 = narrow(g1_wide)
    m1 = inner(d1) * g1
    e1, b1, cc = inner(d1, 2), inner(g1), 2.0 * inner(cond, 2)
    rest1 = inner(m1) + e1 * (b1 - applied(m1, cc))
    middle = rest1 + e1 * prior_m1 + narrow(refine(coarse))
    for _ in range(2):
        earlier = shifted(middle, 2)
        middle = middle + e1 * (b1 + earlier - applied(framed(middle, 1), cc))

    e0 = inner(d0, 2)
    pre = jnp.stack([narrow(inner(rest[0])) + e0 * (e0 * prior_odd), narrow(inner(odd2))])
    state = pre + middle
    sent = shifted(jnp.stack([state[1], e0 * (inner(g[1], 2) + state[0])]), 2)
    state = framed(state, 2, 1)
    ghost = jnp.pad(sent[0], ((1, 1), (0, 0), (0, 0)))

    def swept(v, width):
        return inner(v) - inner(d0, width) * applied(v, inner(cond, width))

    before = jnp.stack([ghost, inner(state[0])])
    state = swept(state, 1) + inner(d0) * (inner(g) + before)
    before = jnp.stack([swept(ghost, 2) + sent[1], inner(state[0])])
    state = swept(state, 2) + e0 * (inner(g, 2) + before)

    def half(v):
        return jnp.where(low, v[..., :HALF, :], v[..., NARROW - HALF :, :])

    both = half(state)
    faces = half(
        jnp.concatenate([sent[0][:1], sent[0][-1:], cond[1:2], cond[-2:-1]])
    )
    keep = jnp.concatenate([jnp.where(low, both[0], both[1]), faces])
    other = flipped(jnp.concatenate([jnp.where(low, both[1], both[0]), faces]), 1)
    full = jnp.concatenate([jnp.where(low, keep, other), jnp.where(low, other, keep)], axis=1)
    state, lead, beyond = full[:planes], full[planes : planes + 2], full[planes + 2 :]
    earlier = shifted(state, 1)
    below, above = exchanged(
        jnp.concatenate([state[-1:], lead[1:]]), jnp.concatenate([state[:1], lead[:1]])
    )
    below, above, earlier = lax.optimization_barrier((below, above, earlier))
    edge = jnp.concatenate([conductivity[:1], conductivity[-1:]])
    de, db = OMEGA / (1.0 + 6.0 * edge), OMEGA / (1.0 + 6.0 * beyond)
    inside = de * edge * (de + db) * jnp.concatenate([below[1:], above[1:]])
    outside = db * beyond * (de + db) * lead
    outside = jnp.where(low, outside, 0.0)

    def spread(v):
        gap = jnp.pad(v[:1], ((0, planes - 1), (0, 0), (0, 0)))
        return gap + jnp.pad(v[1:], ((planes - 1, 0), (0, 0), (0, 0)))

    fix = spread(inside)
    state = state + jnp.where(low, fix, 0.0)
    wide = jnp.concatenate([below[:1] + outside[:1], state, above[:1] + outside[1:]])
    last = source[0] + (earlier + jnp.where(low, 0.0, fix)) - applied(wide, conductivity)
    return state[None], last[None]


def solution(mesh):
    return jax.shard_map(
        body,
        mesh=mesh,
        in_specs=(P("tm", "space", None, None), P("space", None, None)),
        out_specs=(P("tm", "space", None, None), P("tm", "space", None, None)),
        check_vma=False,
    )
```
